32 devices in a mesh: clip: 2 (over x), tile: 16 (over z, y, core).
Axes of the slice: x: 2, y: 2, z: 4, core: 2. Of those that a mesh axis runs over, the one named last changes fastest.
Arguments:
- frames: bfloat16 [8, 32, 128, 1024], P('clip', 'tile'), parts along dimension 0, may hold values from -40 to 40
- keyframes: bfloat16 [4, 32, 128, 1024], P('clip', 'tile'), parts along dimension 0, may hold values from -40 to 40
- matches: int32 [16, 8, 4], P('tile', 'clip'), parts along dimension 1, may hold values from 0 to 5, as said below
- counts: int32 [16, 8], P('tile', 'clip'), parts along dimension 1, may hold values from 1 to 4, as said below
- w_query: bfloat16 [1024, 1024], replicated, may hold values from -1 to 1
- w_key: bfloat16 [1024, 1024], replicated, may hold values from -1 to 1
- w_value: bfloat16 [1024, 1024], replicated, may hold values from -0.1875 to 0.1875
- w_out: bfloat16 [1024, 1024], replicated, may hold values from -0.1875 to 0.1875
Outputs:
- mixed: bfloat16 [8, 32, 128, 1024], P('clip', None, 'tile'), parts along dimension 0
The draws below stay inside these ranges and needn't reach their ends.
There are 2 independent parts, one for each index of `clip`. The reference program is written for one: setup_inputs(seed, part) draws one part's arguments, and reference() takes and returns one part's arrays. A program takes and returns all parts, laid end to end along the dimension named above; an argument that names none is the same for every part. Nothing has to cross between parts.
Inputs may be any that keep to these rules, and one draw needn't show every extreme that they name: `matches`: every entry names a candidate whose block lies inside the image; the entries of one list are distinct, and entry 0 is candidate 1 (keyframe 0's block at the reader's own tile). Entries past the count are valid but unused. `counts`: in every frame some tile uses 4 entries.
All inputs are finite; a program needn't handle non-finite values.
Results may differ from the reference program's by a relative error of at most 0.0095.
Values may be sent and summed in bfloat16 or wider, within the bound.
A program may use at most 128 MiB of HBM per device.

```python
import jax
import jax.numpy as jnp
from jax import lax

D = 1024
HEADS = 16
W = 128
ROWS_DEV = 2
H = 32
FRAMES = 4
KEYS = 2
MAXM = 4
N_TILE = 16


def latent_pair(key):
    base_key = jax.random.fold_in(key, 11)
    frame_key, still_key = jax.random.split(base_key, 2)
    frame_vals = jax.random.normal(frame_key, (FRAMES, H, W, D), jnp.float32)
    still_vals = jax.random.normal(still_key, (KEYS, H, W, D), jnp.float32)
    return (frame_vals, still_vals)


def draw_frames(key, part):
    return latent_pair(key)[0].astype(jnp.bfloat16)


def draw_keyframes(key, part):
    return latent_pair(key)[1].astype(jnp.bfloat16)


def weight_pair(key):
    base_key = jax.random.fold_in(key, 23)
    first_key, second_key = jax.random.split(base_key, 2)
    first_w = jnp.clip(jax.random.normal(first_key, (D, D), jnp.float32), -5.0, 5.0) * D ** (-0.5)
    noise_w = jnp.clip(jax.random.normal(second_key, (D, D), jnp.float32), -5.0, 5.0) * D ** (-0.5)
    second_w = noise_w
    return (first_w, second_w)


def draw_w_query(key, part):
    return weight_pair(key)[0].astype(jnp.bfloat16)


def draw_w_key(key, part):
    return weight_pair(key)[1].astype(jnp.bfloat16)


def draw_matches(key, part):
    match_key = jax.random.fold_in(key, 31)
    cand_total = 3 * KEYS
    scores = jax.random.randint(match_key, (N_TILE, FRAMES, cand_total), 0, 4096, dtype=jnp.int32)
    numbers = jnp.arange(cand_total, dtype=jnp.int32)
    scores = scores * cand_total + numbers[None, None, :]
    tile_ids = jnp.arange(N_TILE, dtype=jnp.int32)[:, None, None]
    target = tile_ids + numbers[None, None, :] % 3 - 1
    inside = (target >= 0) & (target < N_TILE)
    scores = jnp.where(inside, scores + 1, 0)
    scores = jnp.where(numbers[None, None, :] == 1, 4096 * cand_total + 10, scores)
    picked = lax.top_k(scores, MAXM)[1]
    return picked.astype(jnp.int32)


def draw_counts(key, part):
    count_key, busy_key = jax.random.split(jax.random.fold_in(key, 41), 2)
    drawn = jax.random.randint(count_key, (N_TILE, FRAMES), 1, MAXM + 1, dtype=jnp.int32)
    busiest = jax.random.randint(busy_key, (FRAMES,), 0, N_TILE, dtype=jnp.int32)
    tile_ids = jnp.arange(N_TILE, dtype=jnp.int32)[:, None]
    return jnp.where(tile_ids == busiest[None, :], MAXM, drawn).astype(jnp.int32)


def gaussian(key, extent, width, most, kind=jnp.bfloat16):
    return jnp.clip(width * jax.random.normal(key, extent, jnp.float32), -most, most).astype(kind)


def setup_inputs(seed: int = 0, part: int = 0) -> dict:
    splits = jax.random.split(jax.random.key(seed), 9)
    part_splits = jax.random.split(jax.random.fold_in(splits[8], part), 9)
    frames = draw_frames(jax.random.fold_in(jax.random.fold_in(splits[8], part), 71), part)
    keyframes = draw_keyframes(jax.random.fold_in(jax.random.fold_in(splits[8], part), 71), part)
    matches = draw_matches(jax.random.fold_in(jax.random.fold_in(splits[8], part), 71), part)
    counts = draw_counts(jax.random.fold_in(jax.random.fold_in(splits[8], part), 71), part)
    w_query = draw_w_query(jax.random.fold_in(splits[8], 71), part)
    w_key = draw_w_key(jax.random.fold_in(splits[8], 71), part)
    w_value = gaussian(splits[6], (D, D), D ** -0.5, 0.1875)
    w_out = gaussian(splits[7], (D, D), D ** -0.5, 0.1875)
    return {"frames": frames, "keyframes": keyframes, "matches": matches, "counts": counts, "w_query": w_query, "w_key": w_key, "w_value": w_value, "w_out": w_out}


def attend(queries, keys, values, allowed):
    block_len = queries.shape[0]
    head_dim = D // HEADS
    q_heads = queries.reshape(block_len, HEADS, head_dim).astype(jnp.float32)
    k_heads = keys.reshape(-1, HEADS, head_dim).astype(jnp.float32)
    v_heads = values.reshape(-1, HEADS, head_dim).astype(jnp.float32)
    scores = jnp.einsum('qhd,khd->hqk', q_heads, k_heads) * (head_dim ** -0.5)
    scores = jnp.where(allowed[None, None, :], scores, -jnp.inf)
    row_max = jnp.max(scores, axis=-1, keepdims=True)
    exp_terms = jnp.exp(scores - row_max)
    probabilities = (exp_terms / jnp.sum(exp_terms, axis=-1, keepdims=True)).astype(jnp.bfloat16)
    context = jnp.einsum('hqk,khd->qhd', probabilities.astype(jnp.float32), v_heads)
    return context.astype(jnp.bfloat16).reshape(block_len, D)


def reference(frames, keyframes, matches, counts, w_query, w_key, w_value, w_out):
    block_len = ROWS_DEV * W
    query = jnp.dot(frames.reshape(-1, D), w_query, preferred_element_type=jnp.float32).astype(jnp.bfloat16)
    query = query.reshape(FRAMES, N_TILE, block_len, D)
    flat_keys = keyframes.reshape(-1, D)
    key_all = jnp.dot(flat_keys, w_key, preferred_element_type=jnp.float32).astype(jnp.bfloat16)
    value_all = jnp.dot(flat_keys, w_value, preferred_element_type=jnp.float32).astype(jnp.bfloat16)
    key_all = key_all.reshape(KEYS, N_TILE, block_len, D)
    value_all = value_all.reshape(KEYS, N_TILE, block_len, D)
    zero_pad = jnp.zeros((KEYS, 1, block_len, D), jnp.bfloat16)
    key_table = jnp.concatenate([zero_pad, key_all, zero_pad], axis=1)
    value_table = jnp.concatenate([zero_pad, value_all, zero_pad], axis=1)

    def per_item(position):
        tile_id = position // FRAMES
        frame_id = position % FRAMES
        queries = query[frame_id, tile_id]
        candidates = matches[tile_id, frame_id]
        key_id = (candidates // 3).astype(jnp.int32)
        block_id = (tile_id + candidates % 3).astype(jnp.int32)
        keys = key_table[key_id, block_id].reshape(-1, D)
        values = value_table[key_id, block_id].reshape(-1, D)
        live = jnp.arange(MAXM, dtype=jnp.int32) < counts[tile_id, frame_id]
        allowed = jnp.repeat(live, block_len)
        return attend(queries, keys, values, allowed)

    context = lax.map(per_item, jnp.arange(N_TILE * FRAMES, dtype=jnp.int32))
    context = context.reshape(N_TILE, FRAMES, block_len, D).transpose(1, 0, 2, 3).reshape(-1, D)
    update = jnp.dot(context, w_out, preferred_element_type=jnp.float32)
    mixed = frames.reshape(-1, D).astype(jnp.float32) + update
    return mixed.astype(jnp.bfloat16).reshape(FRAMES, H, W, D)
```

```python
import functools

import jax
import jax.numpy as jnp
from jax import lax
from jax.experimental import pallas as pl
from jax.experimental.pallas import tpu as pltpu
from jax.sharding import PartitionSpec as P

HEADS = 16
PAIR = 128
CHUNK = 256
F32 = jnp.float32
BF16 = jnp.bfloat16


def kernel(
    tiles, exchange, col_count,
    matches, counts, frames_in, keys_in, wq_in, wk_in, wv_in, wo_in,
    out,
    frames, stills, wq, wk, wv, wo, queries, key_table, value_table, context, stage,
    load_sem, halo_send, halo_recv, send_sem, recv_sem, own_sem,
):
    frame_count, block_len, model_dim = frames.shape
    key_count = stills.shape[1] // block_len
    slot_count = matches.shape[2]
    head_dim = model_dim // HEADS
    pair_count = model_dim // PAIR
    chunk_count = model_dim // CHUNK
    rows = block_len // col_count
    cols = col_count // tiles
    me = lax.axis_index("tile")

    loads = [
        pltpu.make_async_copy(src, dst, load_sem.at[i])
        for i, (src, dst) in enumerate(
            [
                (wq_in, wq), (frames_in, frames), (keys_in, stills.at[1]),
                (wk_in, wk), (wv_in, wv), (wo_in, wo),
            ]
        )
    ]
    for load in loads:
        load.start()

    barrier = pltpu.get_barrier_semaphore()

    def greet(step, carry):
        other = lax.rem(me + step, tiles)
        pl.semaphore_signal(
            barrier, inc=1, device_id={"tile": other}, device_id_type=pl.DeviceIdType.MESH
        )
        return carry

    lax.fori_loop(1, tiles, greet, 0)
    pl.semaphore_wait(barrier, tiles - 1)

    def halo(slot, other):
        return pltpu.make_async_remote_copy(
            src_ref=keys_in, dst_ref=stills.at[slot],
            send_sem=halo_send.at[slot], recv_sem=halo_recv.at[slot],
            device_id={"tile": other}, device_id_type=pl.DeviceIdType.MESH,
        )

    @pl.when(me < tiles - 1)
    def _():
        halo(0, me + 1).start()

    @pl.when(me > 0)
    def _():
        halo(2, me - 1).start()

    def fill(block, carry):
        one = jnp.where(block < 3 * key_count, 1.0, 0.0).astype(BF16)
        for pair in range(pair_count):
            value_table[block, :, pl.ds(pair * 2 * PAIR + PAIR, PAIR)] = jnp.full(
                (block_len, PAIR), 1.0, F32
            ).astype(BF16) * one
        return carry

    lax.fori_loop(0, 3 * key_count + 1, fill, 0)
    for pair in range(pair_count):
        value_table[3 * key_count, :, pl.ds(pair * 2 * PAIR, PAIR)] = jnp.zeros(
            (block_len, PAIR), BF16
        )

    loads[0].wait()
    loads[1].wait()
    lane = lax.broadcasted_iota(jnp.int32, (block_len, CHUNK), 1)
    even = lax.rem(lane, PAIR) < head_dim

    def project_queries(step, carry):
        frame, chunk = step // chunk_count, lax.rem(step, chunk_count)
        at = pl.ds(pl.multiple_of(chunk * CHUNK, CHUNK), CHUNK)
        q = jnp.dot(frames[frame], wq[:, at], preferred_element_type=F32)
        q = q * head_dim ** (-0.5)
        queries[frame, 0:block_len, at] = jnp.where(even, q, 0.0).astype(BF16)
        queries[frame, block_len : 2 * block_len, at] = jnp.where(even, 0.0, q).astype(BF16)
        return carry

    lax.fori_loop(0, frame_count * chunk_count, project_queries, 0)

    def project_stills(slot):
        def step(chunk, carry):
            at = pl.ds(pl.multiple_of(chunk * CHUNK, CHUNK), CHUNK)
            k = jnp.dot(stills[slot], wk[:, at], preferred_element_type=F32).astype(BF16)
            v = jnp.dot(stills[slot], wv[:, at], preferred_element_type=F32).astype(BF16)
            for key in range(key_count):
                part = slice(key * block_len, (key + 1) * block_len)
                block = slot * key_count + key
                key_table[block, :, at] = k[part]
                for pair in range(CHUNK // PAIR):
                    to = pl.multiple_of(chunk * 2 * CHUNK + pair * 2 * PAIR, PAIR)
                    value_table[block, :, pl.ds(to, PAIR)] = v[part, pair * PAIR : (pair + 1) * PAIR]
            return carry

        lax.fori_loop(0, chunk_count, step, 0)

    for load in loads[2:5]:
        load.wait()
    project_stills(1)

    @pl.when(me > 0)
    def _():
        halo(0, me - 1).wait_recv()
        project_stills(0)

    @pl.when(me < tiles - 1)
    def _():
        halo(2, me + 1).wait_recv()
        project_stills(2)

    loads[5].wait()
    pair_lane = lax.broadcasted_iota(jnp.int32, (block_len, PAIR), 1) < head_dim

    def send(frame, other, source):
        return pltpu.make_async_remote_copy(
            src_ref=stage.at[frame, other], dst_ref=out.at[frame, source],
            send_sem=send_sem.at[frame, other], recv_sem=recv_sem.at[frame, source],
            device_id={"tile": other}, device_id_type=pl.DeviceIdType.MESH,
        )

    def keep(frame):
        return pltpu.make_async_copy(stage.at[frame, me], out.at[frame, me], own_sem.at[frame])

    def one_frame(frame, carry):
        key_at, value_at = [], []
        for slot in range(slot_count):
            used = slot < counts[0, frame]
            chosen = jnp.where(used, matches[0, frame, slot], matches[0, frame, 0])
            block = lax.rem(chosen, 3) * key_count + lax.div(chosen, 3)
            key_at.append(block)
            value_at.append(jnp.where(used, block, 3 * key_count))

        def one_pair(pair, carry):
            at = pl.ds(pl.multiple_of(pair * PAIR, PAIR), PAIR)
            wide = pl.ds(pl.multiple_of(pair * 2 * PAIR, 2 * PAIR), 2 * PAIR)
            halves = []
            for half in range(2):
                q = queries[frame, half * block_len : (half + 1) * block_len, at]
                scores = [
                    lax.dot_general(
                        q, key_table[k, :, at], (((1,), (1,)), ((), ())), preferred_element_type=F32
                    )
                    for k in key_at
                ]
                row_max = jnp.max(functools.reduce(jnp.maximum, scores), axis=1, keepdims=True)
                total = None
                for score, v in zip(scores, value_at):
                    p = jnp.exp(score - row_max).astype(BF16)
                    term = jnp.dot(p, value_table[v, :, wide], preferred_element_type=F32)
                    total = term if total is None else total + term
                halves.append(total[:, :PAIR] / total[:, PAIR:])
            context[:, at] = jnp.where(pair_lane, halves[0], halves[1]).astype(BF16)
            return carry

        lax.fori_loop(0, pair_count, one_pair, 0)

        for chunk in range(chunk_count):
            at = slice(chunk * CHUNK, (chunk + 1) * CHUNK)
            update = jnp.dot(context[...], wo[:, at], preferred_element_type=F32)
            mixed = frames[frame, :, at].astype(F32) + update
            if exchange:
                for other in range(tiles):
                    piece = [
                        mixed[row * col_count + other * cols : row * col_count + (other + 1) * cols]
                        for row in range(rows)
                    ]
                    stage[frame, other, :, at] = jnp.concatenate(piece, axis=0).astype(BF16)
            else:
                stage[frame, 0, :, at] = mixed.astype(BF16)

        if exchange:

            def start(step, carry):
                send(frame, lax.rem(me + step, tiles), me).start()
                return carry

            lax.fori_loop(1, tiles, start, 0)
            keep(frame).start()
        else:
            pltpu.make_async_copy(stage.at[frame, 0], out.at[frame], own_sem.at[frame]).start()
        return carry

    lax.fori_loop(0, frame_count, one_frame, 0)

    @pl.when(me < tiles - 1)
    def _():
        halo(0, me + 1).wait_send()

    @pl.when(me > 0)
    def _():
        halo(2, me - 1).wait_send()

    def finish(frame, carry):
        if exchange:

            def end(step, carry):
                other = lax.rem(me + step, tiles)
                send(frame, other, me).wait_send()
                send(frame, other, other).wait_recv()
                return carry

            lax.fori_loop(1, tiles, end, 0)
            keep(frame).wait()
        else:
            pltpu.make_async_copy(stage.at[frame, 0], out.at[frame], own_sem.at[frame]).wait()
        return carry

    lax.fori_loop(0, frame_count, finish, 0)


def shards(tiles, frames, keyframes, matches, counts, w_query, w_key, w_value, w_out):
    frame_count, row_count, col_count, model_dim = frames.shape
    key_count = keyframes.shape[0]
    block_len = row_count * col_count
    slots = matches.shape[2]
    cols = col_count // tiles
    exchange = cols % 8 == 0
    pieces = tiles if exchange else 1
    piece_len = block_len // pieces
    if exchange:
        out_shape = (frame_count, tiles, piece_len, model_dim)
    else:
        out_shape = (frame_count, block_len, model_dim)
    weight = pltpu.VMEM((model_dim, model_dim), BF16)
    products = (4 * frame_count + 12 * key_count) * block_len * model_dim * model_dim
    products += 4 * frame_count * slots * block_len * block_len * model_dim
    mixed = pl.pallas_call(
        functools.partial(kernel, tiles, exchange, col_count),
        out_shape=jax.ShapeDtypeStruct(out_shape, BF16),
        in_specs=[pl.BlockSpec(memory_space=pltpu.SMEM)] * 2 + [pl.BlockSpec(memory_space=pl.ANY)] * 6,
        out_specs=pl.BlockSpec(memory_space=pl.ANY),
        scratch_shapes=[
            pltpu.VMEM((frame_count, block_len, model_dim), BF16),
            pltpu.VMEM((3, key_count * block_len, model_dim), BF16),
            weight, weight, weight, weight,
            pltpu.VMEM((frame_count, 2 * block_len, model_dim), BF16),
            pltpu.VMEM((3 * key_count, block_len, model_dim), BF16),
            pltpu.VMEM((3 * key_count + 1, block_len, 2 * model_dim), BF16),
            pltpu.VMEM((block_len, model_dim), BF16),
            pltpu.VMEM((frame_count, pieces, piece_len, model_dim), BF16),
            pltpu.SemaphoreType.DMA((6,)),
            pltpu.SemaphoreType.DMA((3,)),
            pltpu.SemaphoreType.DMA((3,)),
            pltpu.SemaphoreType.DMA((frame_count, pieces)),
            pltpu.SemaphoreType.DMA((frame_count, pieces)),
            pltpu.SemaphoreType.DMA((frame_count,)),
        ],
        compiler_params=pltpu.CompilerParams(
            collective_id=0, has_side_effects=True, vmem_limit_bytes=52 * 1024 * 1024
        ),
        cost_estimate=pl.CostEstimate(
            flops=products, bytes_accessed=16 * 1024 * 1024,
            transcendentals=frame_count * slots * HEADS * block_len * block_len,
        ),
        name="attend_and_relay",
    )(
        matches, counts,
        frames.reshape(frame_count, block_len, model_dim),
        keyframes.reshape(key_count * block_len, model_dim),
        w_query, w_key, w_value, w_out,
    )
    if exchange:
        return mixed.reshape(frame_count, tiles * row_count, cols, model_dim)
    mixed = mixed.reshape(frame_count, row_count, col_count, model_dim)
    return lax.all_to_all(mixed, "tile", split_axis=2, concat_axis=1, tiled=True)


def solution(mesh):
    placed = (
        P("clip", "tile", None, None),
        P("clip", "tile", None, None),
        P("tile", "clip", None),
        P("tile", "clip"),
        P(),
        P(),
        P(),
        P(),
    )
    return jax.shard_map(
        functools.partial(shards, mesh.shape["tile"]),
        mesh=mesh, in_specs=placed, out_specs=P("clip", None, "tile", None), check_vma=False,
    )
```

```python
import functools

import jax
import jax.numpy as jnp
from jax import lax
from jax.experimental import pallas as pl
from jax.experimental.pallas import tpu as pltpu
from jax.sharding import PartitionSpec as P

HEADS = 16
PAIR = 128
EARLY_QUERIES = 1
CHUNK = 512
F32 = jnp.float32
BF16 = jnp.bfloat16


def kernel(
    tiles, exchange, col_count,
    matches_in, counts_in, frames_in, keys_in, wq_in, wk_in, wv_in, wo_in,
    out,
    matches, counts, frames, stills, wq, wk, wv, wo, queries, key_table, value_table, context,
    stage, scores_even, scores_odd, max_even, max_odd, early_total, early_max,
    load_sem, halo_send, halo_recv, send_sem, recv_sem, own_sem,
):
    frame_count, block_len, model_dim = frames.shape
    key_count = stills.shape[1] // block_len
    slot_count = matches.shape[2]
    head_dim = model_dim // HEADS
    pair_count = model_dim // PAIR
    chunk_count = model_dim // CHUNK
    rows = block_len // col_count
    cols = col_count // tiles
    me = lax.axis_index("tile")

    loads = [
        pltpu.make_async_copy(src, dst, load_sem.at[i])
        for i, (src, dst) in enumerate(
            [
                (wq_in, wq), (frames_in, frames), (keys_in, stills.at[1]),
                (wk_in, wk), (wv_in, wv), (wo_in, wo),
                (matches_in, matches), (counts_in, counts),
            ]
        )
    ]
    for load in loads:
        load.start()

    barrier = pltpu.get_barrier_semaphore()

    def greet(step, carry):
        other = lax.rem(me + step, tiles)
        pl.semaphore_signal(
            barrier, inc=1, device_id={"tile": other}, device_id_type=pl.DeviceIdType.MESH
        )
        return carry

    lax.fori_loop(1, tiles, greet, 0)
    pl.semaphore_wait(barrier, tiles - 1)

    odd = lax.rem(me, 2)
    partners = ((me + 1 - 2 * odd, 2 - 2 * odd), (me - 1 + 2 * odd, 2 * odd))
    far = partners[1][0]
    has_far = (far >= 0) & (far < tiles)

    def halo(kind, key):
        part = pl.ds(key * block_len, block_len)
        return pltpu.make_async_remote_copy(
            src_ref=keys_in.at[part], dst_ref=stills.at[partners[1 - kind][1], part],
            send_sem=halo_send.at[kind, key], recv_sem=halo_recv.at[kind, key],
            device_id={"tile": partners[kind][0]}, device_id_type=pl.DeviceIdType.MESH,
        )

    def arrival(kind, key):
        part = pl.ds(key * block_len, block_len)
        return pltpu.make_async_remote_copy(
            src_ref=keys_in.at[part], dst_ref=stills.at[partners[kind][1], part],
            send_sem=halo_send.at[kind, key], recv_sem=halo_recv.at[kind, key],
            device_id={"tile": partners[kind][0]}, device_id_type=pl.DeviceIdType.MESH,
        )

    @pl.when(has_far)
    def _():
        for key in range(key_count):
            halo(1, key).start()

    for key in range(key_count):
        halo(0, key).start()

    def fill(block, carry):
        one = jnp.where(block < 3 * key_count, 1.0, 0.0).astype(BF16)
        for pair in range(pair_count):
            value_table[block, :, pl.ds(pair * 2 * PAIR + PAIR, PAIR)] = jnp.full(
                (block_len, PAIR), 1.0, F32
            ).astype(BF16) * one
        return carry

    lax.fori_loop(0, 3 * key_count + 1, fill, 0)
    for pair in range(pair_count):
        value_table[3 * key_count, :, pl.ds(pair * 2 * PAIR, PAIR)] = jnp.zeros(
            (block_len, PAIR), BF16
        )

    loads[0].wait()
    loads[1].wait()
    lane = lax.broadcasted_iota(jnp.int32, (block_len, CHUNK), 1)
    even = lax.rem(lane, PAIR) < head_dim

    def project_queries(frame):
        def step(chunk, carry):
            at = pl.ds(pl.multiple_of(chunk * CHUNK, CHUNK), CHUNK)
            q = jnp.dot(frames[frame], wq[:, at], preferred_element_type=F32)
            q = q * head_dim ** (-0.5)
            queries[frame, 0:block_len, at] = jnp.where(even, q, 0.0).astype(BF16)
            queries[frame, block_len : 2 * block_len, at] = jnp.where(even, 0.0, q).astype(BF16)
            return carry

        lax.fori_loop(0, chunk_count, step, 0)

    for frame in range(EARLY_QUERIES):
        project_queries(frame)

    def project_stills(slot, first, count):
        def step(chunk, carry):
            at = pl.ds(pl.multiple_of(chunk * CHUNK, CHUNK), CHUNK)
            tokens = stills[slot, first * block_len : (first + count) * block_len, :]
            k = jnp.dot(tokens, wk[:, at], preferred_element_type=F32).astype(BF16)
            v = jnp.dot(tokens, wv[:, at], preferred_element_type=F32).astype(BF16)
            for key in range(count):
                part = slice(key * block_len, (key + 1) * block_len)
                block = slot * key_count + first + key
                key_table[block, :, at] = k[part]
                for pair in range(CHUNK // PAIR):
                    to = pl.multiple_of(chunk * 2 * CHUNK + pair * 2 * PAIR, PAIR)
                    value_table[block, :, pl.ds(to, PAIR)] = v[part, pair * PAIR : (pair + 1) * PAIR]
            return carry

        lax.fori_loop(0, chunk_count, step, 0)

    for load in loads[2:5]:
        load.wait()
    project_stills(1, 0, key_count)
    for key in range(key_count):
        arrival(0, key).wait_recv()
    project_stills(partners[0][1], 0, key_count)

    for load in loads[5:]:
        load.wait()
    pair_lane = lax.broadcasted_iota(jnp.int32, (block_len, PAIR), 1) < head_dim

    def send(frame, other, source):
        return pltpu.make_async_remote_copy(
            src_ref=stage.at[frame, other], dst_ref=out.at[frame, source],
            send_sem=send_sem.at[frame, other], recv_sem=recv_sem.at[frame, source],
            device_id={"tile": other}, device_id_type=pl.DeviceIdType.MESH,
        )

    def partner(step):
        if tiles & (tiles - 1):
            return lax.rem(me + step, tiles)
        other, bit = 0, 1
        while bit < tiles:
            other = other + lax.rem(me // bit + step // bit, 2) * bit
            bit *= 2
        return other

    def keep(frame):
        return pltpu.make_async_copy(stage.at[frame, me], out.at[frame, me], own_sem.at[frame])

    def attend(frame, keys, values, early=False, late=False):
        def score(pair, half, scores, top):
            at = pl.ds(pl.multiple_of(pair * PAIR, PAIR), PAIR)
            q = queries[frame, half * block_len : (half + 1) * block_len, at]
            most = None
            for slot, key in enumerate(keys):
                s = lax.dot_general(
                    q, key_table[key, :, at], (((1,), (1,)), ((), ())), preferred_element_type=F32
                )
                scores[:, slot * block_len : (slot + 1) * block_len] = s
                for piece in range(block_len // PAIR):
                    part = s[:, piece * PAIR : (piece + 1) * PAIR]
                    most = part if most is None else jnp.maximum(most, part)
            most = jnp.broadcast_to(jnp.max(most, axis=1, keepdims=True), top.shape)
            if late:
                most = jnp.maximum(most, early_max[pair * 2 + half])
            top[...] = most

        def gather(pair, half, scores, top):
            wide = pl.ds(pl.multiple_of(pair * 2 * PAIR, 2 * PAIR), 2 * PAIR)
            most = top[...]
            total = None
            if late:
                scale = jnp.exp(early_max[pair * 2 + half] - most)
                total = early_total[pair * 2 + half] * jnp.concatenate([scale, scale], axis=1)
            p = jnp.concatenate(
                [
                    jnp.exp(scores[:, at : at + PAIR] - most).astype(BF16)
                    for at in range(0, len(values) * block_len, PAIR)
                ],
                axis=1,
            )
            v = jnp.concatenate([value_table[value, :, wide] for value in values], axis=0)
            term = jnp.dot(p, v, preferred_element_type=F32)
            total = term if total is None else total + term
            if early:
                early_total[pair * 2 + half] = total
                early_max[pair * 2 + half] = most
                return None
            return total[:, :PAIR] / total[:, PAIR:]

        score(0, 0, scores_even, max_even)

        def one_pair(pair, carry):
            at = pl.ds(pl.multiple_of(pair * PAIR, PAIR), PAIR)
            score(pair, 1, scores_odd, max_odd)
            first = gather(pair, 0, scores_even, max_even)
            score(jnp.minimum(pair + 1, pair_count - 1), 0, scores_even, max_even)
            second = gather(pair, 1, scores_odd, max_odd)
            if not early:
                context[:, at] = jnp.where(pair_lane, first, second).astype(BF16)
            return carry

        lax.fori_loop(0, pair_count, one_pair, 0)

    def used(frame, slot):
        return slot < counts[0, frame]

    def named(frame, position):
        keys, values = [], []
        for key in range(key_count):
            there = jnp.int32(0)
            for slot in range(slot_count):
                same = (matches[0, frame, slot] == key * 3 + position) & used(frame, slot)
                there = there + jnp.where(same, 1, 0)
            block = position * key_count + key
            keys.append(jnp.where(there > 0, block, key_count))
            values.append(jnp.where(there > 0, block, 3 * key_count))
        return keys, values

    def finish_frame(frame):
        for chunk in range(chunk_count):
            at = slice(chunk * CHUNK, (chunk + 1) * CHUNK)
            update = jnp.dot(context[...], wo[:, at], preferred_element_type=F32)
            mixed = frames[frame, :, at].astype(F32) + update
            if exchange:
                for other in range(tiles):
                    piece = [
                        mixed[row * col_count + other * cols : row * col_count + (other + 1) * cols]
                        for row in range(rows)
                    ]
                    stage[frame, other, :, at] = jnp.concatenate(piece, axis=0).astype(BF16)
            else:
                stage[frame, 0, :, at] = mixed.astype(BF16)

        if exchange:

            def start(step, carry):
                send(frame, partner(tiles - step), me).start()
                return carry

            lax.fori_loop(1, tiles, start, 0)
            keep(frame).start()
        else:
            pltpu.make_async_copy(stage.at[frame, 0], out.at[frame], own_sem.at[frame]).start()

    def one_frame(frame, carry):
        keys, values = [], []
        for slot in range(slot_count):
            chosen = jnp.where(used(frame, slot), matches[0, frame, slot], matches[0, frame, 0])
            block = lax.rem(chosen, 3) * key_count + lax.div(chosen, 3)
            keys.append(block)
            values.append(jnp.where(used(frame, slot), block, 3 * key_count))
        if EARLY_QUERIES < frame_count:

            @pl.when(frame >= EARLY_QUERIES)
            def _():
                project_queries(frame)

        attend(frame, keys, values)
        finish_frame(frame)
        return carry

    own_keys, own_values = named(0, 1)
    near_keys, near_values = named(0, partners[0][1])
    attend(0, own_keys + near_keys, own_values + near_values, early=True)

    @pl.when(has_far)
    def _():
        for key in range(key_count):
            arrival(1, key).wait_recv()
            project_stills(partners[1][1], key, 1)

    attend(0, *named(0, partners[1][1]), late=True)
    finish_frame(0)
    lax.fori_loop(1, frame_count, one_frame, 0)

    @pl.when(has_far)
    def _():
        for key in range(key_count):
            halo(1, key).wait_send()

    for key in range(key_count):
        halo(0, key).wait_send()

    def finish(frame, carry):
        if exchange:

            def end(step, carry):
                other = lax.rem(me + step, tiles)
                send(frame, other, me).wait_send()
                send(frame, other, other).wait_recv()
                return carry

            lax.fori_loop(1, tiles, end, 0)
            keep(frame).wait()
        else:
            pltpu.make_async_copy(stage.at[frame, 0], out.at[frame], own_sem.at[frame]).wait()
        return carry

    lax.fori_loop(0, frame_count, finish, 0)


def shards(tiles, frames, keyframes, matches, counts, w_query, w_key, w_value, w_out):
    frame_count, row_count, col_count, model_dim = frames.shape
    key_count = keyframes.shape[0]
    block_len = row_count * col_count
    slots = matches.shape[2]
    cols = col_count // tiles
    exchange = cols % 8 == 0
    pieces = tiles if exchange else 1
    piece_len = block_len // pieces
    if exchange:
        out_shape = (frame_count, tiles, piece_len, model_dim)
    else:
        out_shape = (frame_count, block_len, model_dim)
    weight = pltpu.VMEM((model_dim, model_dim), BF16)
    products = (4 * frame_count + 12 * key_count) * block_len * model_dim * model_dim
    products += 4 * frame_count * slots * block_len * block_len * model_dim
    mixed = pl.pallas_call(
        functools.partial(kernel, tiles, exchange, col_count),
        out_shape=jax.ShapeDtypeStruct(out_shape, BF16),
        in_specs=[pl.BlockSpec(memory_space=pl.ANY)] * 8,
        out_specs=pl.BlockSpec(memory_space=pl.ANY),
        scratch_shapes=[
            pltpu.SMEM(matches.shape, jnp.int32),
            pltpu.SMEM(counts.shape, jnp.int32),
            pltpu.VMEM((frame_count, block_len, model_dim), BF16),
            pltpu.VMEM((3, key_count * block_len, model_dim), BF16),
            weight, weight, weight, weight,
            pltpu.VMEM((frame_count, 2 * block_len, model_dim), BF16),
            pltpu.VMEM((3 * key_count, block_len, model_dim), BF16),
            pltpu.VMEM((3 * key_count + 1, block_len, 2 * model_dim), BF16),
            pltpu.VMEM((block_len, model_dim), BF16),
            pltpu.VMEM((frame_count, pieces, piece_len, model_dim), BF16),
            pltpu.VMEM((block_len, slots * block_len), F32),
            pltpu.VMEM((block_len, slots * block_len), F32),
            pltpu.VMEM((block_len, PAIR), F32),
            pltpu.VMEM((block_len, PAIR), F32),
            pltpu.VMEM((HEADS, block_len, 2 * PAIR), F32),
            pltpu.VMEM((HEADS, block_len, PAIR), F32),
            pltpu.SemaphoreType.DMA((8,)),
            pltpu.SemaphoreType.DMA((2, key_count)),
            pltpu.SemaphoreType.DMA((2, key_count)),
            pltpu.SemaphoreType.DMA((frame_count, pieces)),
            pltpu.SemaphoreType.DMA((frame_count, pieces)),
            pltpu.SemaphoreType.DMA((frame_count,)),
        ],
        compiler_params=pltpu.CompilerParams(
            collective_id=0, has_side_effects=True, vmem_limit_bytes=60 * 1024 * 1024
        ),
        cost_estimate=pl.CostEstimate(
            flops=products, bytes_accessed=16 * 1024 * 1024,
            transcendentals=frame_count * slots * HEADS * block_len * block_len,
        ),
        name="attend_and_relay",
    )(
        matches, counts,
        frames.reshape(frame_count, block_len, model_dim),
        keyframes.reshape(key_count * block_len, model_dim),
        w_query, w_key, w_value, w_out,
    )
    if exchange:
        return mixed.reshape(frame_count, tiles * row_count, cols, model_dim)
    mixed = mixed.reshape(frame_count, row_count, col_count, model_dim)
    return lax.all_to_all(mixed, "tile", split_axis=2, concat_axis=1, tiled=True)


def solution(mesh):
    placed = (
        P("clip", "tile", None, None),
        P("clip", "tile", None, None),
        P("tile", "clip", None),
        P("tile", "clip"),
        P(),
        P(),
        P(),
        P(),
    )
    return jax.shard_map(
        functools.partial(shards, mesh.shape["tile"]),
        mesh=mesh, in_specs=placed, out_specs=P("clip", None, "tile", None), check_vma=False,
    )
```

```python
import functools

import jax
import jax.numpy as jnp
from jax import lax
from jax.experimental import pallas as pl
from jax.experimental.pallas import tpu as pltpu
from jax.sharding import PartitionSpec as P

HEADS = 16
PAIR = 128
EARLY_QUERIES = 1
CHUNK = 512
F32 = jnp.float32
BF16 = jnp.bfloat16


def kernel(
    tiles, exchange, col_count,
    matches_in, counts_in, frames_in, keys_in, wq_in, wk_in, wv_in, wo_in,
    out,
    matches, counts, frames, stills, wq, wk, wv, wo, queries, key_table, value_table, context,
    stage, scores_even, scores_odd, max_even, max_odd, early_total, early_max,
    load_sem, halo_send, halo_recv, send_sem, recv_sem, own_sem,
):
    frame_count, block_len, model_dim = frames.shape
    key_count = stills.shape[1] // block_len
    slot_count = matches.shape[2]
    head_dim = model_dim // HEADS
    pair_count = model_dim // PAIR
    chunk_count = model_dim // CHUNK
    rows = block_len // col_count
    cols = col_count // tiles
    me = lax.axis_index("tile")

    loads = [
        pltpu.make_async_copy(src, dst, load_sem.at[i])
        for i, (src, dst) in enumerate(
            [
                (wq_in, wq), (frames_in, frames), (keys_in, stills.at[1]),
                (wk_in, wk), (wv_in, wv), (wo_in, wo),
                (matches_in, matches), (counts_in, counts),
            ]
        )
    ]
    for load in loads:
        load.start()

    barrier = pltpu.get_barrier_semaphore()

    def greet(step, carry):
        other = lax.rem(me + step, tiles)
        pl.semaphore_signal(
            barrier, inc=1, device_id={"tile": other}, device_id_type=pl.DeviceIdType.MESH
        )
        return carry

    lax.fori_loop(1, tiles, greet, 0)
    pl.semaphore_wait(barrier, tiles - 1)

    odd = lax.rem(me, 2)
    partners = ((me + 1 - 2 * odd, 2 - 2 * odd), (me - 1 + 2 * odd, 2 * odd))
    far = partners[1][0]
    has_far = (far >= 0) & (far < tiles)

    def halo(kind, key):
        part = pl.ds(key * block_len, block_len)
        return pltpu.make_async_remote_copy(
            src_ref=keys_in.at[part], dst_ref=stills.at[partners[1 - kind][1], part],
            send_sem=halo_send.at[kind, key], recv_sem=halo_recv.at[kind, key],
            device_id={"tile": partners[kind][0]}, device_id_type=pl.DeviceIdType.MESH,
        )

    def arrival(kind, key):
        part = pl.ds(key * block_len, block_len)
        return pltpu.make_async_remote_copy(
            src_ref=keys_in.at[part], dst_ref=stills.at[partners[kind][1], part],
            send_sem=halo_send.at[kind, key], recv_sem=halo_recv.at[kind, key],
            device_id={"tile": partners[kind][0]}, device_id_type=pl.DeviceIdType.MESH,
        )

    @pl.when(has_far)
    def _():
        for key in range(key_count):
            halo(1, key).start()

    for key in range(key_count):
        halo(0, key).start()

    def fill(block, carry):
        one = jnp.where(block < 3 * key_count, 1.0, 0.0).astype(BF16)
        for pair in range(pair_count):
            value_table[block, :, pl.ds(pair * 2 * PAIR + PAIR, PAIR)] = jnp.full(
                (block_len, PAIR), 1.0, F32
            ).astype(BF16) * one
        return carry

    lax.fori_loop(0, 3 * key_count + 1, fill, 0)
    for pair in range(pair_count):
        value_table[3 * key_count, :, pl.ds(pair * 2 * PAIR, PAIR)] = jnp.zeros(
            (block_len, PAIR), BF16
        )

    loads[0].wait()
    loads[1].wait()
    lane = lax.broadcasted_iota(jnp.int32, (block_len, CHUNK), 1)
    even = lax.rem(lane, PAIR) < head_dim

    def project_queries(frame):
        def step(chunk, carry):
            at = pl.ds(pl.multiple_of(chunk * CHUNK, CHUNK), CHUNK)
            q = jnp.dot(frames[frame], wq[:, at], preferred_element_type=F32)
            q = q * head_dim ** (-0.5)
            queries[frame, 0:block_len, at] = jnp.where(even, q, 0.0).astype(BF16)
            queries[frame, block_len : 2 * block_len, at] = jnp.where(even, 0.0, q).astype(BF16)
            return carry

        lax.fori_loop(0, chunk_count, step, 0)

    for frame in range(EARLY_QUERIES):
        project_queries(frame)

    def project_stills(slot, first, count):
        def step(chunk, carry):
            at = pl.ds(pl.multiple_of(chunk * CHUNK, CHUNK), CHUNK)
            tokens = stills[slot, first * block_len : (first + count) * block_len, :]
            k = jnp.dot(tokens, wk[:, at], preferred_element_type=F32).astype(BF16)
            v = jnp.dot(tokens, wv[:, at], preferred_element_type=F32).astype(BF16)
            for key in range(count):
                part = slice(key * block_len, (key + 1) * block_len)
                block = slot * key_count + first + key
                key_table[block, at, :] = k[part].T
                for pair in range(CHUNK // PAIR):
                    to = pl.multiple_of(chunk * 2 * CHUNK + pair * 2 * PAIR, PAIR)
                    value_table[block, :, pl.ds(to, PAIR)] = v[part, pair * PAIR : (pair + 1) * PAIR]
            return carry

        lax.fori_loop(0, chunk_count, step, 0)

    for load in loads[2:5]:
        load.wait()
    project_stills(1, 0, key_count)
    for key in range(key_count):
        arrival(0, key).wait_recv()
    project_stills(partners[0][1], 0, key_count)

    for load in loads[5:]:
        load.wait()
    pair_lane = lax.broadcasted_iota(jnp.int32, (block_len, PAIR), 1) < head_dim

    def send(frame, other, source):
        return pltpu.make_async_remote_copy(
            src_ref=stage.at[frame, other], dst_ref=out.at[frame, source],
            send_sem=send_sem.at[frame, other], recv_sem=recv_sem.at[frame, source],
            device_id={"tile": other}, device_id_type=pl.DeviceIdType.MESH,
        )

    def partner(step):
        if tiles & (tiles - 1):
            return lax.rem(me + step, tiles)
        other, bit = 0, 1
        while bit < tiles:
            other = other + lax.rem(me // bit + step // bit, 2) * bit
            bit *= 2
        return other

    def keep(frame):
        return pltpu.make_async_copy(stage.at[frame, me], out.at[frame, me], own_sem.at[frame])

    def attend(frame, keys, values, early=False, late=False):
        def score_block(q, slot, at, scores, most):
            s = jnp.dot(q, key_table[keys[slot], at, :], preferred_element_type=F32)
            scores[:, slot * block_len : (slot + 1) * block_len] = s
            for piece in range(block_len // PAIR):
                part = s[:, piece * PAIR : (piece + 1) * PAIR]
                most = part if most is None else jnp.maximum(most, part)
            return most

        def value_block(slot, wide, scores, most, total):
            p = jnp.concatenate(
                [
                    jnp.exp(scores[:, at : at + PAIR] - most).astype(BF16)
                    for at in range(slot * block_len, (slot + 1) * block_len, PAIR)
                ],
                axis=1,
            )
            term = jnp.dot(p, value_table[values[slot], :, wide], preferred_element_type=F32)
            return term if total is None else total + term

        def close(most, pair, top):
            most = jnp.broadcast_to(jnp.max(most, axis=1, keepdims=True), top.shape)
            if late:
                most = jnp.maximum(most, early_max[pair])
            top[...] = most

        def columns(pair, width):
            return pl.ds(pl.multiple_of(pair * width, width), width)

        def load_query(pair):
            return queries[frame, :, columns(pair, PAIR)]

        def step(pair, scores, top, next_pair, next_scores, next_top):
            most, total, next_most = top[...], None, None
            q = load_query(next_pair)
            if late:
                scale = jnp.exp(early_max[pair] - most)
                total = early_total[pair] * jnp.concatenate([scale, scale], axis=1)
            for slot in range(len(keys)):
                next_most = score_block(q, slot, columns(next_pair, PAIR), next_scores, next_most)
                total = value_block(slot, columns(pair, 2 * PAIR), scores, most, total)
            close(next_most, next_pair, next_top)
            if early:
                early_total[pair] = total
                early_max[pair] = most
                return None
            each = total[:, :PAIR] / total[:, PAIR:]
            both = jnp.where(pair_lane, each[:block_len], each[block_len:])
            context[:, columns(pair, PAIR)] = both.astype(BF16)

        most, q = None, load_query(0)
        for slot in range(len(keys)):
            most = score_block(q, slot, columns(0, PAIR), scores_even, most)
        close(most, 0, max_even)

        def two_pairs(index, carry):
            pair = index * 2
            after = jnp.minimum(pair + 2, pair_count - 1)
            step(pair, scores_even, max_even, pair + 1, scores_odd, max_odd)
            step(pair + 1, scores_odd, max_odd, after, scores_even, max_even)
            return carry

        lax.fori_loop(0, pair_count // 2, two_pairs, 0)

    def used(frame, slot):
        return slot < counts[0, frame]

    def named(frame, position):
        keys, values = [], []
        for key in range(key_count):
            there = jnp.int32(0)
            for slot in range(slot_count):
                same = (matches[0, frame, slot] == key * 3 + position) & used(frame, slot)
                there = there + jnp.where(same, 1, 0)
            block = position * key_count + key
            keys.append(jnp.where(there > 0, block, key_count))
            values.append(jnp.where(there > 0, block, 3 * key_count))
        return keys, values

    def finish_frame(frame):
        for chunk in range(chunk_count):
            at = slice(chunk * CHUNK, (chunk + 1) * CHUNK)
            update = jnp.dot(context[...], wo[:, at], preferred_element_type=F32)
            mixed = frames[frame, :, at].astype(F32) + update
            if exchange:
                for other in range(tiles):
                    piece = [
                        mixed[row * col_count + other * cols : row * col_count + (other + 1) * cols]
                        for row in range(rows)
                    ]
                    stage[frame, other, :, at] = jnp.concatenate(piece, axis=0).astype(BF16)
            else:
                stage[frame, 0, :, at] = mixed.astype(BF16)

        if exchange:

            def start(step, carry):
                send(frame, partner(tiles - step), me).start()
                return carry

            lax.fori_loop(1, tiles, start, 0)
            keep(frame).start()
        else:
            pltpu.make_async_copy(stage.at[frame, 0], out.at[frame], own_sem.at[frame]).start()

    def one_frame(frame, carry):
        keys, values = [], []
        for slot in range(slot_count):
            chosen = jnp.where(used(frame, slot), matches[0, frame, slot], matches[0, frame, 0])
            block = lax.rem(chosen, 3) * key_count + lax.div(chosen, 3)
            keys.append(block)
            values.append(jnp.where(used(frame, slot), block, 3 * key_count))
        if EARLY_QUERIES < frame_count:

            @pl.when(frame >= EARLY_QUERIES)
            def _():
                project_queries(frame)

        attend(frame, keys, values)
        finish_frame(frame)
        return carry

    own_keys, own_values = named(0, 1)
    near_keys, near_values = named(0, partners[0][1])
    attend(0, own_keys + near_keys, own_values + near_values, early=True)

    @pl.when(has_far)
    def _():
        for key in range(key_count):
            arrival(1, key).wait_recv()
            project_stills(partners[1][1], key, 1)

    attend(0, *named(0, partners[1][1]), late=True)
    finish_frame(0)
    lax.fori_loop(1, frame_count, one_frame, 0)

    @pl.when(has_far)
    def _():
        for key in range(key_count):
            halo(1, key).wait_send()

    for key in range(key_count):
        halo(0, key).wait_send()

    def finish(frame, carry):
        if exchange:

            def end(step, carry):
                other = lax.rem(me + step, tiles)
                send(frame, other, me).wait_send()
                send(frame, other, other).wait_recv()
                return carry

            lax.fori_loop(1, tiles, end, 0)
            keep(frame).wait()
        else:
            pltpu.make_async_copy(stage.at[frame, 0], out.at[frame], own_sem.at[frame]).wait()
        return carry

    lax.fori_loop(0, frame_count, finish, 0)


def shards(tiles, frames, keyframes, matches, counts, w_query, w_key, w_value, w_out):
    frame_count, row_count, col_count, model_dim = frames.shape
    key_count = keyframes.shape[0]
    block_len = row_count * col_count
    slots = matches.shape[2]
    cols = col_count // tiles
    exchange = cols % 8 == 0
    pieces = tiles if exchange else 1
    piece_len = block_len // pieces
    if exchange:
        out_shape = (frame_count, tiles, piece_len, model_dim)
    else:
        out_shape = (frame_count, block_len, model_dim)
    weight = pltpu.VMEM((model_dim, model_dim), BF16)
    products = (4 * frame_count + 12 * key_count) * block_len * model_dim * model_dim
    products += 4 * frame_count * slots * block_len * block_len * model_dim
    mixed = pl.pallas_call(
        functools.partial(kernel, tiles, exchange, col_count),
        out_shape=jax.ShapeDtypeStruct(out_shape, BF16),
        in_specs=[pl.BlockSpec(memory_space=pl.ANY)] * 8,
        out_specs=pl.BlockSpec(memory_space=pl.ANY),
        scratch_shapes=[
            pltpu.SMEM(matches.shape, jnp.int32),
            pltpu.SMEM(counts.shape, jnp.int32),
            pltpu.VMEM((frame_count, block_len, model_dim), BF16),
            pltpu.VMEM((3, key_count * block_len, model_dim), BF16),
            weight, weight, weight, weight,
            pltpu.VMEM((frame_count, 2 * block_len, model_dim), BF16),
            pltpu.VMEM((3 * key_count, model_dim, block_len), BF16),
            pltpu.VMEM((3 * key_count + 1, block_len, 2 * model_dim), BF16),
            pltpu.VMEM((block_len, model_dim), BF16),
            pltpu.VMEM((frame_count, pieces, piece_len, model_dim), BF16),
            pltpu.VMEM((2 * block_len, slots * block_len), F32),
            pltpu.VMEM((2 * block_len, slots * block_len), F32),
            pltpu.VMEM((2 * block_len, PAIR), F32),
            pltpu.VMEM((2 * block_len, PAIR), F32),
            pltpu.VMEM((HEADS // 2, 2 * block_len, 2 * PAIR), F32),
            pltpu.VMEM((HEADS // 2, 2 * block_len, PAIR), F32),
            pltpu.SemaphoreType.DMA((8,)),
            pltpu.SemaphoreType.DMA((2, key_count)),
            pltpu.SemaphoreType.DMA((2, key_count)),
            pltpu.SemaphoreType.DMA((frame_count, pieces)),
            pltpu.SemaphoreType.DMA((frame_count, pieces)),
            pltpu.SemaphoreType.DMA((frame_count,)),
        ],
        compiler_params=pltpu.CompilerParams(
            collective_id=0, has_side_effects=True, vmem_limit_bytes=60 * 1024 * 1024
        ),
        cost_estimate=pl.CostEstimate(
            flops=products, bytes_accessed=16 * 1024 * 1024,
            transcendentals=frame_count * slots * HEADS * block_len * block_len,
        ),
        name="attend_and_relay",
    )(
        matches, counts,
        frames.reshape(frame_count, block_len, model_dim),
        keyframes.reshape(key_count * block_len, model_dim),
        w_query, w_key, w_value, w_out,
    )
    if exchange:
        return mixed.reshape(frame_count, tiles * row_count, cols, model_dim)
    mixed = mixed.reshape(frame_count, row_count, col_count, model_dim)
    return lax.all_to_all(mixed, "tile", split_axis=2, concat_axis=1, tiled=True)


def solution(mesh):
    placed = (
        P("clip", "tile", None, None),
        P("clip", "tile", None, None),
        P("tile", "clip", None),
        P("tile", "clip"),
        P(),
        P(),
        P(),
        P(),
    )
    return jax.shard_map(
        functools.partial(shards, mesh.shape["tile"]),
        mesh=mesh, in_specs=placed, out_specs=P("clip", None, "tile", None), check_vma=False,
    )
```
